32 devices in a mesh: dom: 16 (over z, y, core), mode: 2 (over x).
Axes of the slice: x: 2, y: 2, z: 4, core: 2. Of those that a mesh axis runs over, the one named last changes fastest.
Arguments:
- mode_basis: bfloat16 [3, 512, 16384], P(None, 'mode', 'dom'), may hold values from -6 to 6
- blocks: bfloat16 [16, 3, 3, 16384], P(None, None, None, 'dom'), may hold values from -0.875 to 0.875
- columns: int32 [16, 16384], P(None, 'dom'), may hold values from -256 to 257, as said below
- samples: int32 [512], replicated, may hold values from 0 to 49151, as said below
- inverse: bfloat16 [512, 512], replicated, may hold values from -0.25 to 0.25
Outputs:
- reduced: float32 [512, 512], P('dom', 'mode')
- coefficients: float32 [512, 512], P('dom', 'mode')
The draws below stay inside these ranges and needn't reach their ends.
Inputs may be any that keep to these rules, and one draw needn't show every extreme that they name: `columns`: each entry is 256 + 1 (an empty slot) or an offset that keeps n + offset within 0 to 16383; slot 0 of every row holds offset 0. `samples`: 512 distinct dofs; half of them lie in the first half of the dofs.
All inputs are finite; a program needn't handle non-finite values.
Results may differ from the reference program's by a relative error of at most 0.0029.
Values may be sent and summed in bfloat16 or wider, within the bound.
A program may use at most 64 MiB of HBM per device.

```python
import jax
import jax.numpy as jnp
from jax import lax

R = 512
SAMPLES = 512
NBR = 16
HB = 256
NN = 16384


def draw_columns(key, part):
    first_key, second_key = jax.random.split(jax.random.fold_in(key, 11))
    counts = jax.random.randint(first_key, (1, NN), NBR // 2, NBR + 1)
    offsets = jax.random.randint(second_key, (NBR, NN), -HB, HB + 1)
    slot_index = lax.broadcasted_iota(jnp.int32, (NBR, NN), 0)
    node_index = lax.broadcasted_iota(jnp.int32, (NBR, NN), 1)
    forced = (slot_index == 1) & (node_index == NN - 1)
    offsets = jnp.where(slot_index == 0, 0, offsets)
    offsets = jnp.where(forced, -HB, offsets)
    target = node_index + offsets
    usable = (slot_index < counts) & (target >= 0) & (target < NN)
    usable = usable | forced
    usable = usable & jnp.logical_not((slot_index == NBR - 1) & (node_index == 0))
    return jnp.where(usable, offsets, HB + 1).astype(jnp.int32)


def draw_samples(key, part):
    first_key, second_key = jax.random.split(jax.random.fold_in(key, 23))
    lower_count = 3 * NN // 2
    upper_count = 3 * NN - lower_count
    lower_half = SAMPLES // 2
    lower = jax.random.permutation(first_key, lower_count)[:lower_half]
    lower = (lower - lower[0]) % lower_count
    upper = jax.random.permutation(second_key, upper_count)[:SAMPLES - lower_half]
    upper = 3 * NN - 1 - (upper - upper[0]) % upper_count
    return jnp.concatenate([lower, upper]).astype(jnp.int32)


def block_scale(stream_key, dims, pieces, low, top_value):
    loudness, own = 1.0, jax.random.fold_in(stream_key, 6)
    for axis_at, shards_of in pieces:
        draws = jnp.exp(jax.random.uniform(jax.random.fold_in(own, axis_at), (shards_of,), jnp.float32, low / len(pieces), top_value / len(pieces)))
        loudness = loudness * jnp.repeat(draws, dims[axis_at] // shards_of).reshape([-1 if axis == axis_at else 1 for axis in range(len(dims))])
    return loudness


def bell_draw(key, extent, scale, bound, shards=(), kind=jnp.bfloat16):
    result = jax.random.normal(key, extent, jnp.float32) * scale
    if len(shards) > 0:
        result = block_scale(key, extent, shards, -0.22, 0.18) * result
    return jnp.clip(result, min=-bound, max=bound).astype(kind)


def setup_inputs(seed: int = 0) -> dict:
    streams_of = jax.random.split(jax.random.key(seed), 6)
    mode_basis = bell_draw(streams_of[0], (3, R, NN), 1.0, 6.0, ((1, 2), (2, 16)))
    blocks = bell_draw(streams_of[1], (NBR, 3, 3, NN), (3 * NBR) ** -0.5, 0.875, ((3, 16),))
    columns = draw_columns(jax.random.fold_in(streams_of[5], 71), 0)
    samples = draw_samples(jax.random.fold_in(streams_of[5], 71), 0)
    inverse = bell_draw(streams_of[4], (SAMPLES, SAMPLES), SAMPLES ** -0.5, 0.25)
    return dict(mode_basis=mode_basis, blocks=blocks, columns=columns, samples=samples, inverse=inverse)


def reference(mode_basis, blocks, columns, samples, inverse):
    node_ids = lax.broadcasted_iota(jnp.int32, (NN,), 0)

    def slot_step(slot_index, running):
        offset = columns[slot_index]
        usable = offset != HB + 1
        position = jnp.where(usable, node_ids + offset, 0).astype(jnp.int32)
        nearby = jnp.take(mode_basis, position, axis=2).astype(jnp.float32)
        weights = jnp.where(usable[None, None, :], blocks[slot_index].astype(jnp.float32), jnp.float32(0.0))
        running = running + weights[:, 0, None, :] * nearby[0][None]
        running = running + weights[:, 1, None, :] * nearby[1][None]
        running = running + weights[:, 2, None, :] * nearby[2][None]
        return running
    zero_image = jnp.zeros(mode_basis.shape, jnp.float32)
    image = lax.fori_loop(0, NBR, slot_step, zero_image).astype(jnp.bfloat16)
    reduced = jnp.tensordot(mode_basis.astype(jnp.float32), image.astype(jnp.float32), axes=((0, 2), (0, 2)), precision=lax.Precision.HIGHEST)
    reduced = reduced / jnp.sqrt(jnp.float32(3 * NN))
    component = samples % 3
    node_index = samples // 3
    picked = image[component, :, node_index]
    coefficients = jnp.dot(inverse, picked, preferred_element_type=jnp.float32)
    return (reduced, coefficients)
```

```python
import functools
import math

import jax
import jax.numpy as jnp
from jax import lax
from jax.experimental import pallas as pl
from jax.experimental.pallas import tpu as pltpu
from jax.sharding import PartitionSpec as P

MESH = pl.DeviceIdType.MESH
LANES = 128
ROWS = 64
F32, BF16 = jnp.float32, jnp.bfloat16


def dot_nt(a, b):
    return lax.dot_general(a, b, (((1,), (1,)), ((), ())), preferred_element_type=F32)


def kernel(
    doms, modes, halo, scaling,
    basis, blocks, columns, samples, inverse,
    reduced_out, coef_out,
    ext, other, image, weights, spread, onehot, chosen, coef, part, coef_in, part_in,
    local_sem, halo_send, halo_recv, gather_send, gather_recv,
    coef_send, coef_recv, part_send, part_recv,
):
    slots = columns.shape[0]
    modes_here, nodes = basis.shape[1], basis.shape[2]
    rows = reduced_out.shape[0]
    group = doms // modes
    window = LANES + 2 * halo
    tiles = nodes // LANES
    dom, mode = lax.axis_index("dom"), lax.axis_index("mode")

    def at_dom(target):
        return (target, mode)

    barrier = pltpu.get_barrier_semaphore()

    def greet(step, carry):
        pl.semaphore_signal(barrier, inc=1, device_id=at_dom(lax.rem(dom + step, doms)), device_id_type=MESH)
        return carry

    lax.fori_loop(1, doms, greet, 0)
    for step in range(1, modes):
        pl.semaphore_signal(barrier, inc=1, device_id=(dom, lax.rem(mode + step, modes)), device_id_type=MESH)

    local = pltpu.make_async_copy(basis, ext.at[:, :, pl.ds(halo, nodes)], local_sem)
    local.start()
    pl.semaphore_wait(barrier, doms + modes - 2)

    up = pltpu.make_async_remote_copy(
        basis.at[:, :, pl.ds(nodes - halo, halo)], ext.at[:, :, pl.ds(0, halo)],
        halo_send.at[0], halo_recv.at[0], at_dom(lax.rem(dom + 1, doms)), MESH,
    )
    down = pltpu.make_async_remote_copy(
        basis.at[:, :, pl.ds(0, halo)], ext.at[:, :, pl.ds(halo + nodes, halo)],
        halo_send.at[1], halo_recv.at[1], at_dom(lax.rem(dom + doms - 1, doms)), MESH,
    )

    @pl.when(dom < doms - 1)
    def _():
        up.start()

    @pl.when(dom > 0)
    def _():
        down.start()

    gathers = []
    for c in range(3):
        for step in range(1, modes):
            copy = pltpu.make_async_remote_copy(
                basis.at[c], other.at[step - 1, c],
                gather_send.at[step - 1, c], gather_recv.at[step - 1, c],
                (dom, lax.rem(mode + step, modes)), MESH,
            )
            copy.start()
            gathers.append(copy)

    @pl.when(dom == 0)
    def _():
        ext[:, :, pl.ds(0, halo)] = jnp.zeros((3, modes_here, halo), BF16)

    @pl.when(dom == doms - 1)
    def _():
        ext[:, :, pl.ds(halo + nodes, halo)] = jnp.zeros((3, modes_here, halo), BF16)

    row_ids = (
        lax.broadcasted_iota(jnp.int32, (ROWS // 16, 16, LANES), 0) * 16
        + lax.broadcasted_iota(jnp.int32, (ROWS // 16, 16, LANES), 1)
    ).astype(F32).astype(BF16)
    lane_ids = lax.broadcasted_iota(jnp.int32, (1, LANES), 1)

    def tile_step(step, carry):
        tile = lax.rem(step + tiles // 4, tiles)
        start = pl.multiple_of(tile * LANES, LANES)
        here = pl.ds(start, LANES)

        offsets, values = [], []
        for j in range(slots):
            offset = columns[pl.ds(j, 1), here]
            offsets.append(jnp.where(offset == halo + 1, -8 * halo - j, offset))
            values.append([blocks[j, a, :, here].astype(F32) for a in range(3)])
        for i in range(slots):
            for j in range(i + 1, slots):
                same = offsets[j] == offsets[i]
                for a in range(3):
                    values[i][a] = values[i][a] + jnp.where(same, values[j][a], 0.0)
                offsets[j] = jnp.where(same, -8 * halo - j, offsets[j])
        for j in range(slots):
            for a in range(3):
                for b in range(3):
                    spread[j, 3 * a + b] = jnp.broadcast_to(
                        values[j][a][b:b + 1], (16, LANES)
                    ).astype(BF16)
        places = [(offset + lane_ids + halo).astype(F32) for offset in offsets]

        def row_step(segment, inner):
            base = (segment * ROWS).astype(F32)
            sums = [jnp.zeros((ROWS // 16, 16, LANES), BF16) for _ in range(9)]
            for j in range(slots):
                place = jnp.broadcast_to(places[j] - base, (16, LANES)).astype(BF16)
                hit = row_ids == place[None]
                for k in range(9):
                    sums[k] = jnp.where(hit, spread[j, k][None], sums[k])
            span = pl.ds(pl.multiple_of(segment * ROWS, ROWS), ROWS)
            for a in range(3):
                for b in range(3):
                    weights[b, span, a * LANES:(a + 1) * LANES] = sums[3 * a + b].reshape(ROWS, LANES)
            return inner

        lax.fori_loop(0, window // ROWS, row_step, 0)

        @pl.when(step == 0)
        def _():
            local.wait()

        @pl.when(step == tiles // 2)
        def _():
            @pl.when(dom > 0)
            def _():
                up.wait_recv()

            @pl.when(dom < doms - 1)
            def _():
                down.wait_recv()

        total = jnp.zeros((modes_here, 3 * LANES), F32)
        for b in range(3):
            total = total + jnp.dot(
                ext[b, :, pl.ds(start, window)], weights[b], preferred_element_type=F32
            )
        for a in range(3):
            image[a, :, here] = total[:, a * LANES:(a + 1) * LANES].astype(BF16)
        return carry

    lax.fori_loop(0, tiles, tile_step, 0)

    dofs = samples[...] - 3 * nodes * dom
    sample_count = dofs.shape[1]
    chosen[...] = jnp.zeros_like(chosen)
    node_ids = 3 * lax.broadcasted_iota(jnp.int32, (LANES, sample_count), 0)
    for c in range(3):
        def mark(tile, carry):
            found = node_ids == dofs - (3 * LANES * tile + c)
            onehot[pl.ds(pl.multiple_of(tile * LANES, LANES), LANES), :] = jnp.where(found, 1.0, 0.0).astype(BF16)
            return carry

        lax.fori_loop(0, tiles, mark, 0)
        chosen[...] += jnp.dot(image[c], onehot[...], preferred_element_type=F32)
    coef[...] = dot_nt(inverse[...], chosen[...].astype(BF16))

    def rows_of(target):
        return pl.ds(pl.multiple_of(target * rows, 8), rows)

    def slot_at(target):
        return lax.rem(dom - target + doms, doms) - 1

    def coef_copy(step):
        target = lax.rem(dom + step, doms)
        slot = doms - step - 1
        return pltpu.make_async_remote_copy(
            coef.at[rows_of(target)], coef_in.at[slot], coef_send.at[step - 1], coef_recv.at[slot],
            at_dom(target), MESH,
        )

    def send_coef(step, carry):
        coef_copy(step).start()
        return carry

    lax.fori_loop(1, doms, send_coef, 0)

    def part_copy(target):
        slot = lax.rem(dom - target + doms - 1 + doms, doms)
        return pltpu.make_async_remote_copy(
            part.at[rows_of(target)], part_in.at[slot], part_send.at[target], part_recv.at[slot],
            at_dom(target), MESH,
        )

    def send_parts(block):
        def send(g, carry):
            target = block * group + g

            @pl.when(target != dom)
            def _():
                part_copy(target).start()

            return carry

        lax.fori_loop(0, group, send, 0)

    def block_rows(block):
        return pl.ds(pl.multiple_of(block * modes_here, 8), modes_here)

    total = jnp.zeros((modes_here, modes_here), F32)
    for c in range(3):
        total = total + dot_nt(ext[c, :, pl.ds(halo, nodes)], image[c])
    part[block_rows(mode)] = total
    send_parts(mode)

    for step in range(1, modes):
        block = lax.rem(mode + modes - step, modes)
        total = jnp.zeros((modes_here, modes_here), F32)
        for c in range(3):
            gathers[c * (modes - 1) + step - 1].wait_recv()
            total = total + dot_nt(other[step - 1, c], image[c])
        part[block_rows(block)] = total
        send_parts(block)

    coef_out[...] = coef[rows_of(dom)]
    reduced_out[...] = part[rows_of(dom)]

    def add_coef(step, carry):
        coef_copy(doms - step).wait_recv()
        coef_out[...] += coef_in[step - 1]
        return carry

    lax.fori_loop(1, doms, add_coef, 0)

    def add_part(step, carry):
        pltpu.make_async_remote_copy(
            part.at[rows_of(0)], part_in.at[step - 1], part_send.at[0], part_recv.at[step - 1],
            at_dom(lax.rem(dom + 1, doms)), MESH,
        ).wait_recv()
        reduced_out[...] += part_in[step - 1]
        return carry

    lax.fori_loop(1, doms, add_part, 0)
    reduced_out[...] = reduced_out[...] * scaling

    for copy in gathers:
        copy.wait_send()

    @pl.when(dom < doms - 1)
    def _():
        up.wait_send()

    @pl.when(dom > 0)
    def _():
        down.wait_send()

    def end_coef(step, carry):
        coef_copy(step).wait_send()
        return carry

    lax.fori_loop(1, doms, end_coef, 0)

    def end_part(target, carry):
        @pl.when(target != dom)
        def _():
            part_copy(target).wait_send()

        return carry

    lax.fori_loop(0, doms, end_part, 0)


def solution(mesh):
    doms, modes = mesh.shape["dom"], mesh.shape["mode"]

    def shards(mode_basis, blocks, columns, samples, inverse):
        modes_here, nodes = mode_basis.shape[1:]
        halo = nodes // 4
        count = inverse.shape[0]
        mode_rows, coef_rows = modes * modes_here // doms, count // doms
        scaling = 1.0 / math.sqrt(3 * nodes * doms)
        vmem = pl.BlockSpec(memory_space=pltpu.VMEM)
        dma = pltpu.SemaphoreType.DMA
        return pl.pallas_call(
            functools.partial(kernel, doms, modes, halo, scaling),
            out_shape=(
                jax.ShapeDtypeStruct((mode_rows, modes_here), F32),
                jax.ShapeDtypeStruct((coef_rows, modes_here), F32),
            ),
            in_specs=[pl.BlockSpec(memory_space=pl.ANY), vmem, vmem, vmem, vmem],
            out_specs=(vmem, vmem),
            scratch_shapes=[
                pltpu.VMEM((3, modes_here, nodes + 2 * halo), BF16),
                pltpu.VMEM((modes - 1, 3, modes_here, nodes), BF16),
                pltpu.VMEM((3, modes_here, nodes), BF16),
                pltpu.VMEM((3, LANES + 2 * halo, 3 * LANES), BF16),
                pltpu.VMEM((blocks.shape[0], 9, 16, LANES), BF16),
                pltpu.VMEM((nodes, count), BF16),
                pltpu.VMEM((modes_here, count), F32),
                pltpu.VMEM((count, modes_here), F32),
                pltpu.VMEM((modes * modes_here, modes_here), F32),
                pltpu.VMEM((doms - 1, coef_rows, modes_here), F32),
                pltpu.VMEM((doms - 1, mode_rows, modes_here), F32),
                dma, dma((2,)), dma((2,)), dma((modes - 1, 3)), dma((modes - 1, 3)),
                dma((doms - 1,)), dma((doms - 1,)), dma((doms,)), dma((doms - 1,)),
            ],
            compiler_params=pltpu.CompilerParams(
                collective_id=0, has_side_effects=True, vmem_limit_bytes=48 * 1024 * 1024
            ),
        )(mode_basis, blocks, columns, samples.reshape(1, count), inverse)

    return jax.shard_map(
        shards,
        mesh=mesh,
        in_specs=(P(None, "mode", "dom"), P(None, None, None, "dom"), P(None, "dom"), P(), P()),
        out_specs=(P("dom", "mode"), P("dom", "mode")),
        check_vma=False,
    )
```

```python
import functools
import math

import jax
import jax.numpy as jnp
from jax import lax
from jax.experimental import pallas as pl
from jax.experimental.pallas import tpu as pltpu
from jax.sharding import PartitionSpec as P

MESH = pl.DeviceIdType.MESH
LANES = 128
ROWS = 64
F32, BF16 = jnp.float32, jnp.bfloat16


def dot_nt(a, b):
    return lax.dot_general(a, b, (((1,), (1,)), ((), ())), preferred_element_type=F32)


def kernel(
    doms, modes, halo, scaling,
    basis, blocks_hbm, columns_hbm, samples_hbm, inverse_hbm,
    reduced_out, coef_out,
    blocks, columns, samples, inverse, ext, other, image, weights, spread, onehot, chosen, coef, part, coef_in, part_in, coef_twin, part_twin,
    local_sem, load_sem, halo_send, halo_recv, gather_send, gather_recv,
    coef_send, coef_recv, part_send, part_recv, twin_send, twin_recv,
):
    slots = columns.shape[0]
    modes_here, nodes = basis.shape[1], basis.shape[2]
    rows = reduced_out.shape[0]
    chunks = doms // modes // 2
    chunk = modes_here // chunks
    window = LANES + 2 * halo
    tiles = nodes // LANES
    dom, mode = lax.axis_index("dom"), lax.axis_index("mode")

    def at_dom(target):
        return (target, mode)

    barrier = pltpu.get_barrier_semaphore()

    def greet(step, carry):
        pl.semaphore_signal(barrier, inc=1, device_id=at_dom(lax.rem(dom + step, doms)), device_id_type=MESH)
        return carry

    lax.fori_loop(1, doms, greet, 0)
    for step in range(1, modes):
        pl.semaphore_signal(barrier, inc=1, device_id=(dom, lax.rem(mode + step, modes)), device_id_type=MESH)

    local = pltpu.make_async_copy(basis, ext.at[:, :, pl.ds(halo, nodes)], local_sem)
    loads = [
        pltpu.make_async_copy(columns_hbm, columns, load_sem.at[0]),
        pltpu.make_async_copy(blocks_hbm, blocks, load_sem.at[1]),
        pltpu.make_async_copy(samples_hbm, samples, load_sem.at[2]),
        pltpu.make_async_copy(inverse_hbm, inverse, load_sem.at[3]),
    ]
    for load in loads[:2]:
        load.start()
    local.start()
    for load in loads[2:]:
        load.start()
    pl.semaphore_wait(barrier, doms + modes - 2)

    up = pltpu.make_async_remote_copy(
        basis.at[:, :, pl.ds(nodes - halo, halo)], ext.at[:, :, pl.ds(0, halo)],
        halo_send.at[0], halo_recv.at[0], at_dom(lax.rem(dom + 1, doms)), MESH,
    )
    down = pltpu.make_async_remote_copy(
        basis.at[:, :, pl.ds(0, halo)], ext.at[:, :, pl.ds(halo + nodes, halo)],
        halo_send.at[1], halo_recv.at[1], at_dom(lax.rem(dom + doms - 1, doms)), MESH,
    )

    @pl.when(dom < doms - 1)
    def _():
        up.start()

    @pl.when(dom > 0)
    def _():
        down.start()

    gathers = []
    spans = [
        pl.ds(pl.multiple_of(lax.rem(dom // 2 + piece, chunks) * chunk, 16), chunk) for piece in range(chunks)
    ]
    for step in range(1, modes):
        for piece in range(chunks):
            copy = pltpu.make_async_remote_copy(
                basis.at[:, spans[piece]], other.at[step - 1, :, spans[piece]],
                gather_send.at[step - 1, piece], gather_recv.at[step - 1, piece],
                (dom, lax.rem(mode + step, modes)), MESH,
            )
            copy.start()
            gathers.append(copy)

    @pl.when(dom == 0)
    def _():
        ext[:, :, pl.ds(0, halo)] = jnp.zeros((3, modes_here, halo), BF16)

    @pl.when(dom == doms - 1)
    def _():
        ext[:, :, pl.ds(halo + nodes, halo)] = jnp.zeros((3, modes_here, halo), BF16)

    row_ids = (
        lax.broadcasted_iota(jnp.int32, (ROWS // 16, 16, LANES), 0) * 16
        + lax.broadcasted_iota(jnp.int32, (ROWS // 16, 16, LANES), 1)
    ).astype(F32).astype(BF16)
    lane_ids = lax.broadcasted_iota(jnp.int32, (slots, LANES), 1)
    slot_ids = lax.broadcasted_iota(jnp.int32, (slots, LANES), 0)
    unused = -8 * halo - slot_ids
    loads[0].wait()
    loads[1].wait()

    def tile_step(step, carry):
        tile = lax.rem(step + tiles // 4, tiles)
        start = pl.multiple_of(tile * LANES, LANES)
        here = pl.ds(start, LANES)

        offsets = columns[:, here]
        offsets = jnp.where(offsets == halo + 1, unused, offsets)
        values = [blocks[k // 3, k % 3, :, here].astype(F32) for k in range(9)]
        sums = list(values)
        repeated = offsets < -16 * halo
        for shift in range(1, slots):
            later = pltpu.roll(offsets, slots - shift, 0)
            same = (later == offsets) & (slot_ids < slots - shift)
            for k in range(9):
                sums[k] = sums[k] + jnp.where(same, pltpu.roll(values[k], slots - shift, 0), 0.0)
            earlier = pltpu.roll(offsets, shift, 0)
            repeated = repeated | ((earlier == offsets) & (slot_ids >= shift))
        offsets = jnp.where(repeated, unused, offsets)
        for j in range(slots):
            for k in range(9):
                spread[j, k] = jnp.broadcast_to(sums[k][j:j + 1], (16, LANES)).astype(BF16)
        places = (offsets + lane_ids + halo).astype(F32)

        def row_step(segment, inner):
            base = (segment * ROWS).astype(F32)
            sums = [jnp.zeros((ROWS // 16, 16, LANES), BF16) for _ in range(9)]
            for j in range(slots):
                place = jnp.broadcast_to(places[j:j + 1] - base, (16, LANES)).astype(BF16)
                hit = row_ids == place[None]
                for k in range(9):
                    sums[k] = jnp.where(hit, spread[j, k][None], sums[k])
            span = pl.ds(pl.multiple_of(segment * ROWS, ROWS), ROWS)
            for a in range(3):
                for b in range(3):
                    weights[b, span, a * LANES:(a + 1) * LANES] = sums[3 * a + b].reshape(ROWS, LANES)
            return inner

        lax.fori_loop(0, window // ROWS, row_step, 0)

        @pl.when(step == 0)
        def _():
            local.wait()

        @pl.when(step == tiles // 2)
        def _():
            @pl.when(dom > 0)
            def _():
                up.wait_recv()

            @pl.when(dom < doms - 1)
            def _():
                down.wait_recv()

        total = jnp.zeros((modes_here, 3 * LANES), F32)
        for b in range(3):
            total = total + jnp.dot(
                ext[b, :, pl.ds(start, window)], weights[b], preferred_element_type=F32
            )
        for a in range(3):
            image[a, :, here] = total[:, a * LANES:(a + 1) * LANES].astype(BF16)
        return carry

    lax.fori_loop(0, tiles, tile_step, 0)

    loads[2].wait()
    loads[3].wait()

    dofs = samples[...] - 3 * nodes * dom
    sample_count = dofs.shape[1]
    chosen[...] = jnp.zeros_like(chosen)
    node_ids = 3 * lax.broadcasted_iota(jnp.int32, (LANES, sample_count), 0)
    for c in range(3):
        def mark(tile, carry):
            found = node_ids == dofs - (3 * LANES * tile + c)
            onehot[pl.ds(pl.multiple_of(tile * LANES, LANES), LANES), :] = jnp.where(found, 1.0, 0.0).astype(BF16)
            return carry

        lax.fori_loop(0, tiles, mark, 0)
        chosen[...] += jnp.dot(image[c], onehot[...], preferred_element_type=F32)
    share = dot_nt(inverse[...], chosen[...].astype(BF16))
    for target in range(doms):
        coef[target % 2, pl.ds(target // 2 * rows, rows)] = share[target * rows:(target + 1) * rows]

    pairs = doms // 2
    pair, side = dom // 2, lax.rem(dom, 2)
    twin = dom + 1 - 2 * side

    def rows_of(target_pair):
        return pl.ds(pl.multiple_of(target_pair * rows, 8), rows)

    coef_swap = pltpu.make_async_remote_copy(
        coef.at[1 - side], coef_twin, twin_send.at[pairs], twin_recv.at[pairs], at_dom(twin), MESH,
    )
    coef_swap.start()

    def part_swap(target):
        return pltpu.make_async_remote_copy(
            part.at[1 - side, rows_of(target)], part_twin.at[rows_of(target)],
            twin_send.at[target], twin_recv.at[target], at_dom(twin), MESH,
        )

    def share_copy(source, landing, send, recv, step):
        target = lax.rem(pair + step, pairs)
        slot = pairs - step - 1
        return pltpu.make_async_remote_copy(
            source.at[side, rows_of(target)], landing.at[slot], send.at[step - 1], recv.at[slot],
            at_dom(2 * target + side), MESH,
        )

    def coef_copy(step):
        return share_copy(coef, coef_in, coef_send, coef_recv, step)

    def part_copy(step):
        return share_copy(part, part_in, part_send, part_recv, step)

    def begin(target, total):
        part[0, rows_of(target)] = total[:rows]
        part[1, rows_of(target)] = total[rows:]
        part_swap(target).start()

    def finish(target):
        swap = part_swap(target)
        swap.wait_recv()
        swap.wait_send()
        part[side, rows_of(target)] += part_twin[rows_of(target)]

        @pl.when(target != pair)
        def _():
            part_copy(lax.rem(target - pair + pairs, pairs)).start()

    total = jnp.zeros((modes_here, modes_here), F32)
    for c in range(3):
        total = total + dot_nt(ext[c, :, pl.ds(halo, nodes)], image[c])
    for place in range(chunks):
        begin(mode * chunks + place, total[place * chunk:(place + 1) * chunk])

    coef_swap.wait_recv()
    coef_swap.wait_send()
    coef[side] += coef_twin[...]

    def send_coef(step, carry):
        coef_copy(step).start()
        return carry

    lax.fori_loop(1, pairs, send_coef, 0)
    for place in range(chunks):
        finish(mode * chunks + place)

    pending = None
    for step in range(1, modes):
        block = lax.rem(mode + modes - step, modes)
        for piece in range(chunks):
            gathers[(step - 1) * chunks + piece].wait_recv()
            total = jnp.zeros((chunk, modes_here), F32)
            for c in range(3):
                total = total + dot_nt(other[step - 1, c, spans[piece]], image[c])
            target = block * chunks + lax.rem(pair + piece, chunks)
            begin(target, total)
            if pending is not None:
                finish(pending)
            pending = target
    if pending is not None:
        finish(pending)

    coef_out[...] = coef[side, rows_of(pair)]
    reduced_out[...] = part[side, rows_of(pair)]

    def add_coef(step, carry):
        coef_copy(pairs - step).wait_recv()
        coef_out[...] += coef_in[step - 1]
        return carry

    lax.fori_loop(1, pairs, add_coef, 0)

    def add_part(step, carry):
        part_copy(pairs - step).wait_recv()
        reduced_out[...] += part_in[step - 1]
        return carry

    lax.fori_loop(1, pairs, add_part, 0)
    reduced_out[...] = reduced_out[...] * scaling

    for copy in gathers:
        copy.wait_send()

    @pl.when(dom < doms - 1)
    def _():
        up.wait_send()

    @pl.when(dom > 0)
    def _():
        down.wait_send()

    def end_shares(step, carry):
        coef_copy(step).wait_send()
        part_copy(step).wait_send()
        return carry

    lax.fori_loop(1, pairs, end_shares, 0)


def solution(mesh):
    doms, modes = mesh.shape["dom"], mesh.shape["mode"]

    def shards(mode_basis, blocks, columns, samples, inverse):
        modes_here, nodes = mode_basis.shape[1:]
        halo = nodes // 4
        count = inverse.shape[0]
        mode_rows, coef_rows = modes * modes_here // doms, count // doms
        scaling = 1.0 / math.sqrt(3 * nodes * doms)
        vmem = pl.BlockSpec(memory_space=pltpu.VMEM)
        dma = pltpu.SemaphoreType.DMA
        return pl.pallas_call(
            functools.partial(kernel, doms, modes, halo, scaling),
            out_shape=(
                jax.ShapeDtypeStruct((mode_rows, modes_here), F32),
                jax.ShapeDtypeStruct((coef_rows, modes_here), F32),
            ),
            in_specs=[pl.BlockSpec(memory_space=pltpu.HBM)] * 5,
            out_specs=(vmem, vmem),
            scratch_shapes=[
                pltpu.VMEM((3, 3, blocks.shape[0], nodes), BF16),
                pltpu.VMEM(columns.shape, jnp.int32),
                pltpu.VMEM((1, count), jnp.int32),
                pltpu.VMEM(inverse.shape, BF16),
                pltpu.VMEM((3, modes_here, nodes + 2 * halo), BF16),
                pltpu.VMEM((modes - 1, 3, modes_here, nodes), BF16),
                pltpu.VMEM((3, modes_here, nodes), BF16),
                pltpu.VMEM((3, LANES + 2 * halo, 3 * LANES), BF16),
                pltpu.VMEM((blocks.shape[0], 9, 16, LANES), BF16),
                pltpu.VMEM((nodes, count), BF16),
                pltpu.VMEM((modes_here, count), F32),
                pltpu.VMEM((2, count // 2, modes_here), F32),
                pltpu.VMEM((2, modes * modes_here // 2, modes_here), F32),
                pltpu.VMEM((doms // 2 - 1, coef_rows, modes_here), F32),
                pltpu.VMEM((doms // 2 - 1, mode_rows, modes_here), F32),
                pltpu.VMEM((count // 2, modes_here), F32),
                pltpu.VMEM((modes * modes_here // 2, modes_here), F32),
                dma, dma((4,)), dma((2,)), dma((2,)), dma((modes - 1, doms // modes // 2)), dma((modes - 1, doms // modes // 2)),
                *[dma((doms // 2 - 1,))] * 4, *[dma((doms // 2 + 1,))] * 2,
            ],
            compiler_params=pltpu.CompilerParams(
                collective_id=0, has_side_effects=True, vmem_limit_bytes=62 * 1024 * 1024
            ),
        )(mode_basis, jnp.transpose(blocks, (1, 2, 0, 3)), columns, samples.reshape(1, count), inverse)

    return jax.shard_map(
        shards,
        mesh=mesh,
        in_specs=(P(None, "mode", "dom"), P(None, None, None, "dom"), P(None, "dom"), P(), P()),
        out_specs=(P("dom", "mode"), P("dom", "mode")),
        check_vma=False,
    )
```
